32 devices in a mesh: groups: 2 (over y), tm: 4 (over z), pair: 2 (over x), head: 2 (over core).
Axes of the slice: x: 2, y: 2, z: 4, core: 2. Of those that a mesh axis runs over, the one named last changes fastest.
Arguments:
- gdn_query: bfloat16 [4, 512, 8, 128], P(('groups', 'pair'), 'tm', 'head'), parts along dimension 0, may hold values from -14 to 14
- gdn_key: bfloat16 [4, 512, 8, 128], P(('groups', 'pair'), 'tm', 'head'), parts along dimension 0, may hold values from -12 to 12
- gdn_value: bfloat16 [4, 512, 8, 128], P(('groups', 'pair'), 'tm', 'head'), parts along dimension 0, may hold values from -0.59765625 to 0.59765625
- log_decay: float32 [4, 8, 512], P(('groups', 'pair'), 'head', 'tm'), parts along dimension 0, may hold values from -0.8 to 0
- write_rate: float32 [4, 8, 512], P(('groups', 'pair'), 'head', 'tm'), parts along dimension 0, may hold values from 0.025 to 0.05
- init_state: float32 [4, 8, 128, 128], P(('groups', 'pair'), 'head'), parts along dimension 0, may hold values from -0.5 to 0.5
- attn_query: bfloat16 [4, 512, 8, 128], P(('groups', 'pair'), 'tm', 'head'), parts along dimension 0, may hold values from -6 to 6
- attn_key: bfloat16 [4, 512, 2, 128], P(('groups', 'pair'), 'tm', 'head'), parts along dimension 0, may hold values from -6 to 6
- attn_value: bfloat16 [4, 512, 2, 128], P(('groups', 'pair'), 'tm', 'head'), parts along dimension 0, may hold values from -6 to 6
- readout: bfloat16 [4, 512, 8, 128], P(('groups', 'pair'), 'tm', 'head'), parts along dimension 0, may hold values from -0.1875 to 0.1875
- speaker_mask: int32 [4, 512], P(('groups', 'pair'), 'tm'), parts along dimension 0, may hold values 0 or 1
- pair_slot: int32 [4], P(('groups', 'pair')), parts along dimension 0, may hold values from 0 to 1, each once
- ref_margin: float32 [2], P('groups'), parts along dimension 0, may hold values from -4 to 4
Outputs:
- dpo_loss: float32 [2], P('groups'), parts along dimension 0
- grad_gdn_query: bfloat16 [4, 512, 8, 128], P(('groups', 'pair'), 'tm', 'head'), parts along dimension 0
- grad_gdn_key: bfloat16 [4, 512, 8, 128], P(('groups', 'pair'), 'tm', 'head'), parts along dimension 0
- grad_gdn_value: bfloat16 [4, 512, 8, 128], P(('groups', 'pair'), 'tm', 'head'), parts along dimension 0
- grad_log_decay: float32 [4, 8, 512], P(('groups', 'pair'), 'head', 'tm'), parts along dimension 0
- grad_write_rate: float32 [4, 8, 512], P(('groups', 'pair'), 'head', 'tm'), parts along dimension 0
- grad_attn_query: bfloat16 [4, 512, 8, 128], P(('groups', 'pair'), 'tm', 'head'), parts along dimension 0
- grad_attn_key: bfloat16 [4, 512, 2, 128], P(('groups', 'pair'), 'tm', 'head'), parts along dimension 0
- grad_attn_value: bfloat16 [4, 512, 2, 128], P(('groups', 'pair'), 'tm', 'head'), parts along dimension 0
The draws below stay inside these ranges and needn't reach their ends.
There are 2 independent parts, one for each index of `groups`. The reference program is written for one: setup_inputs(seed, part) draws one part's arguments, and reference() takes and returns one part's arrays. A program takes and returns all parts, laid end to end along the dimension named above; each array names one. Nothing has to cross between parts.
Inputs may be any that keep to these rules, and one draw needn't show every extreme that they name: `pair_slot`: a permutation of 0 to 1; slot // 2 names the pair, an even slot the chosen rollout.
All inputs are finite; a program needn't handle non-finite values. No bound on the sum of `speaker_mask` on one device may be relied on, other than what follows from the above.
Results may differ from the reference program's by a relative error of at most 0.011.
Values may be sent and summed in bfloat16 or wider, within the bound.
A program may use at most 128 MiB of HBM per device.

```python
import math
import jax
import jax.numpy as jnp
from jax import lax

MIXER_HEADS = 8
KVH = 2
DH = 128
BLOCK = 64
WIN = 512
TLEN = 128
SEQUENCE_FRAMES = 512
ROLLOUT_COUNT = 2
NPAIRS = 1


def shared_direction(key):
    return jax.random.truncated_normal(jax.random.fold_in(key, 41), -3.0, 3.0, (ROLLOUT_COUNT, 1, MIXER_HEADS, DH), jnp.float32)


def draw_gdn_query(key, part):
    direction = shared_direction(key)
    key = jax.random.fold_in(key, 42)
    shape = (ROLLOUT_COUNT, SEQUENCE_FRAMES, MIXER_HEADS, DH)
    noise = jax.random.truncated_normal(key, -5.0, 5.0, shape, jnp.float32)
    weight = 3.5
    return jnp.clip(noise + weight * direction, -14.0, 14.0).astype(jnp.bfloat16)


def draw_gdn_key(key, part):
    direction = shared_direction(key)
    key = jax.random.fold_in(key, 43)
    shape = (ROLLOUT_COUNT, SEQUENCE_FRAMES, MIXER_HEADS, DH)
    noise = jax.random.truncated_normal(key, -5.0, 5.0, shape, jnp.float32)
    weight = 3.0
    return jnp.clip(noise + weight * direction, -12.0, 12.0).astype(jnp.bfloat16)


def draw_log_decay(key, part):
    slow_share = 0.5
    slow_heads = jax.random.bernoulli(jax.random.fold_in(key, 1), slow_share, (ROLLOUT_COUNT, MIXER_HEADS, 1))
    baseline_rate = jnp.where(slow_heads, 0.25 / SEQUENCE_FRAMES, 1.0 / 40.0)
    jaggedness = jnp.exp(jax.random.uniform(jax.random.fold_in(key, 2), (ROLLOUT_COUNT, MIXER_HEADS, SEQUENCE_FRAMES), jnp.float32, -0.69, 0.69))
    dispersion = jnp.exp(jax.random.uniform(jax.random.fold_in(key, 3), (ROLLOUT_COUNT, MIXER_HEADS, SEQUENCE_FRAMES // TLEN), jnp.float32, -0.69, 0.69))
    dispersion = jnp.repeat(dispersion, TLEN, axis=2)
    spike_events = jax.random.bernoulli(jax.random.fold_in(key, 4), 2.0 / SEQUENCE_FRAMES, (ROLLOUT_COUNT, 1, SEQUENCE_FRAMES))
    spike_loss = jnp.log(jax.random.uniform(jax.random.fold_in(key, 5), (ROLLOUT_COUNT, MIXER_HEADS, SEQUENCE_FRAMES), jnp.float32, 0.5, 0.8))
    return -baseline_rate * jaggedness * dispersion + jnp.where(spike_events, spike_loss, 0.0)


def query_key_pair(key):
    query_shape = (ROLLOUT_COUNT, SEQUENCE_FRAMES, MIXER_HEADS, DH)
    key_shape = (ROLLOUT_COUNT, SEQUENCE_FRAMES, KVH, DH)
    queries = jax.random.truncated_normal(jax.random.fold_in(key, 21), -6.0, 6.0, query_shape, jnp.float32)
    key_rows = jax.random.truncated_normal(jax.random.fold_in(key, 22), -6.0, 6.0, key_shape, jnp.float32)
    return (queries, key_rows)


def draw_attn_query(key, part):
    return query_key_pair(key)[0].astype(jnp.bfloat16)


def draw_attn_key(key, part):
    return query_key_pair(key)[1].astype(jnp.bfloat16)


def set_ends(array, own_key, low, largest):
    longest = array.shape.index(max(array.shape))
    spots = []
    for shift in (0, 1):
        where = [jax.random.randint(jax.random.fold_in(own_key, axis), (), 0, length) for axis, length in enumerate(array.shape)]
        where[longest] = (where[longest] + shift) % array.shape[longest]
        spots.append(tuple(where))
    return array.at[spots[0]].set(low).at[spots[1]].set(largest)


def level_of(key, dims, cuts, low, top_value):
    gain, own = 1.0, jax.random.fold_in(key, 6)
    for axis_at, parts in cuts:
        heights = jnp.exp(jax.random.uniform(jax.random.fold_in(own, axis_at), (parts,), jnp.float32, low / len(cuts), top_value / len(cuts)))
        gain = gain * jnp.repeat(heights, dims[axis_at] // parts).reshape([-1 if axis == axis_at else 1 for axis in range(len(dims))])
    return gain


def centred(own_key, shape, scale, limit, split=(), kind=jnp.bfloat16):
    drawn = scale * jax.random.normal(own_key, shape, jnp.float32)
    if split:
        drawn = drawn * level_of(own_key, shape, split, -0.22, 0.18)
    return jnp.clip(drawn, -limit, limit).astype(kind)


def setup_inputs(seed: int = 0, part: int = 0) -> dict:
    seeds = jax.random.split(jax.random.key(seed), 14)
    own_keys = jax.random.split(jax.random.fold_in(seeds[13], part), 14)
    gdn_query = draw_gdn_query(jax.random.fold_in(jax.random.fold_in(seeds[13], part), 71), part)
    gdn_key = draw_gdn_key(jax.random.fold_in(jax.random.fold_in(seeds[13], part), 71), part)
    gdn_value = centred(own_keys[2], (ROLLOUT_COUNT, SEQUENCE_FRAMES, MIXER_HEADS, DH), 0.1, 0.59765625, ((0, 2), (1, 4), (2, 2)))
    log_decay = draw_log_decay(jax.random.fold_in(jax.random.fold_in(seeds[13], part), 71), part)
    write_rate = jnp.clip(jnp.exp(math.log(0.05) - 0.6931472 * jax.random.uniform(own_keys[4], (ROLLOUT_COUNT, MIXER_HEADS, SEQUENCE_FRAMES), jnp.float32) ** level_of(own_keys[4], (ROLLOUT_COUNT, MIXER_HEADS, SEQUENCE_FRAMES), ((0, 2), (1, 2), (2, 4)), -0.2, 0.2)), 0.025, 0.05)
    init_state = jnp.clip(jax.random.uniform(own_keys[5], (ROLLOUT_COUNT, MIXER_HEADS, DH, DH), jnp.float32, -0.5, 0.5) * level_of(own_keys[5], (ROLLOUT_COUNT, MIXER_HEADS, DH, DH), ((0, 2), (1, 2)), -0.4, 0.0), -0.5, 0.5)
    attn_query = draw_attn_query(jax.random.fold_in(jax.random.fold_in(seeds[13], part), 71), part)
    attn_key = draw_attn_key(jax.random.fold_in(jax.random.fold_in(seeds[13], part), 71), part)
    attn_value = centred(own_keys[8], (ROLLOUT_COUNT, SEQUENCE_FRAMES, KVH, DH), 1.0, 6.0, ((0, 2), (1, 4), (2, 2)))
    readout = centred(own_keys[9], (ROLLOUT_COUNT, SEQUENCE_FRAMES, MIXER_HEADS, DH), (MIXER_HEADS * DH) ** -0.5, 0.1875, ((0, 2), (1, 4), (2, 2)))
    speaker_mask = set_ends((jax.random.randint(own_keys[10], (ROLLOUT_COUNT, SEQUENCE_FRAMES), 0, 2) < 1).astype(jnp.int32), jax.random.fold_in(own_keys[10], 1), 0, 1)
    pair_slot = jax.random.permutation(own_keys[11], ROLLOUT_COUNT).astype(jnp.int32)
    ref_margin = centred(own_keys[12], (NPAIRS,), 1.0, 4.0, (), jnp.float32)
    return dict(gdn_query=gdn_query, gdn_key=gdn_key, gdn_value=gdn_value, log_decay=log_decay, write_rate=write_rate, init_state=init_state, attn_query=attn_query, attn_key=attn_key, attn_value=attn_value, readout=readout, speaker_mask=speaker_mask, pair_slot=pair_slot, ref_margin=ref_margin)


HIGH = lax.Precision.HIGHEST
EPSILON = 1e-06

def unit_lower_inverse(strict_part):
    block_size = strict_part.shape[-1]
    identity = jnp.eye(block_size, dtype=jnp.float32)
    power_term = -strict_part
    result = identity + power_term
    for doubling_step in range(1, (block_size - 1).bit_length()):
        power_term = jnp.einsum('...ij,...jk->...ik', power_term, power_term, precision=HIGH)
        result = jnp.einsum('...ij,...jk->...ik', result, identity + power_term, precision=HIGH)
    return result

def normalize_rows(source):
    return source * lax.rsqrt(lax.optimization_barrier(jnp.sum(source * source, axis=-1, keepdims=True)) + EPSILON)

def block_step(carried, pieces):
    queries, key_rows, values, log_gate, write_gate = pieces
    block_size = log_gate.shape[-1]
    positions = jnp.arange(block_size, dtype=jnp.int32)
    on_or_below = positions[:, None] >= positions[None, :]
    strict = positions[:, None] > positions[None, :]
    cumulative = jnp.cumsum(log_gate, axis=-1)
    log_gaps = jnp.where(on_or_below, cumulative[..., :, None] - cumulative[..., None, :], 0.0)
    decays = jnp.where(on_or_below, jnp.exp(log_gaps), 0.0)
    key_key = jnp.einsum('shcd,shed->shce', key_rows, key_rows, precision=HIGH)
    strict_part = jnp.where(strict, write_gate[..., :, None] * decays * key_key, 0.0)
    inverse = unit_lower_inverse(strict_part)
    leading = jnp.exp(cumulative)
    key_state = jnp.einsum('shcd,shde->shce', key_rows, carried, precision=HIGH)
    target = write_gate[..., None] * (values - leading[..., None] * key_state)
    deltas = jnp.einsum('shce,shef->shcf', inverse, target, precision=HIGH)
    query_key = jnp.einsum('shcd,shed->shce', queries, key_rows, precision=HIGH)
    from_state = jnp.einsum('shcd,shde->shce', queries, carried, precision=HIGH)
    outputs = leading[..., None] * from_state + jnp.einsum('shce,shef->shcf', decays * query_key, deltas, precision=HIGH)
    tail_decay = jnp.exp(cumulative[..., -1:] - cumulative)
    new_state = jnp.exp(cumulative[..., -1])[..., None, None] * carried + jnp.einsum('shcd,shcf->shdf', key_rows * tail_decay[..., None], deltas, precision=HIGH)
    return (new_state, outputs)

def run_blocks(carried, queries, key_rows, values, log_gate, write_gate):
    seq_count, head_count, length, feature_width = queries.shape
    block_count = length // BLOCK

    def to_blocks(source):
        shaped = source.reshape(source.shape[:2] + (block_count, BLOCK) + source.shape[3:])
        return jnp.moveaxis(shaped, 2, 0)
    final_state, outputs = lax.scan(block_step, carried, (to_blocks(queries), to_blocks(key_rows), to_blocks(values), to_blocks(log_gate), to_blocks(write_gate)))
    outputs = jnp.moveaxis(outputs, 0, 2).reshape(seq_count, head_count, length, feature_width)
    return (outputs, final_state)

def gdn_mixer(queries, key_rows, values, log_gate, write_gate, carried):
    normal_queries = jnp.swapaxes(normalize_rows(queries), 1, 2)
    normal_keys = jnp.swapaxes(normalize_rows(key_rows), 1, 2)
    value_rows = jnp.swapaxes(values, 1, 2)
    raw_out, final_state = run_blocks(carried, normal_queries, normal_keys, value_rows, log_gate, write_gate)
    raw_out = jnp.swapaxes(raw_out, 1, 2)
    scaled = raw_out * lax.rsqrt(lax.optimization_barrier(jnp.mean(raw_out * raw_out, axis=-1, keepdims=True)) + EPSILON)
    return (scaled, final_state)

def window_softmax(query_group, key_window, query_start, key_start):
    score_scale = key_window.shape[-1] ** (-0.5)
    scores = jnp.einsum('stgrd,swgd->sgrtw', query_group, key_window, preferred_element_type=jnp.float32) * score_scale
    query_pos = query_start + jnp.arange(query_group.shape[1], dtype=jnp.int32)
    key_pos = key_start + jnp.arange(key_window.shape[1], dtype=jnp.int32)
    allowed = (key_pos[None, :] <= query_pos[:, None]) & (key_pos[None, :] > query_pos[:, None] - WIN) & (key_pos[None, :] >= 0)
    scores = jnp.where(allowed, scores, -jnp.inf)
    row_max = lax.optimization_barrier(jnp.max(scores, axis=-1, keepdims=True))
    shifted = jnp.exp(scores - row_max)
    return shifted / lax.optimization_barrier(jnp.sum(shifted, axis=-1, keepdims=True))

def window_backward(query_group, key_window, value_window, soft_weights, out_grad, attn_out):
    score_scale = key_window.shape[-1] ** (-0.5)
    grad_low = out_grad.astype(jnp.bfloat16)
    weights = soft_weights.astype(jnp.bfloat16)
    grad_prob = jnp.einsum('stgrd,swgd->sgrtw', grad_low, value_window, preferred_element_type=jnp.float32)
    row_term = jnp.moveaxis(lax.optimization_barrier(jnp.sum(out_grad * attn_out, axis=-1)), 1, 3)
    grad_score = (soft_weights * (grad_prob - row_term[..., None]) * score_scale).astype(jnp.bfloat16)
    grad_query = jnp.einsum('sgrtw,swgd->stgrd', grad_score, key_window, preferred_element_type=jnp.float32)
    grad_key = jnp.einsum('sgrtw,stgrd->swgd', grad_score, query_group, preferred_element_type=jnp.float32)
    grad_value = jnp.einsum('sgrtw,stgrd->swgd', weights, grad_low, preferred_element_type=jnp.float32)
    return (grad_query, grad_key, grad_value)

def reference(gdn_query, gdn_key, gdn_value, log_decay, write_rate, init_state, attn_query, attn_key, attn_value, readout, speaker_mask, pair_slot, ref_margin):
    group_size = MIXER_HEADS // KVH
    block_rows = math.gcd(SEQUENCE_FRAMES, 512)
    block_count = SEQUENCE_FRAMES // block_rows
    query_f = gdn_query.astype(jnp.float32)
    key_f = gdn_key.astype(jnp.float32)
    value_f = gdn_value.astype(jnp.float32)

    def mixer_one(inputs):
        part_query, part_key, part_value, part_decay, part_rate, part_state = inputs
        mixed, final_state = gdn_mixer(part_query[None], part_key[None], part_value[None], part_decay[None], part_rate[None], part_state[None])
        return mixed[0]
    gdn_out = lax.map(mixer_one, (query_f, key_f, value_f, log_decay, write_rate, init_state))

    def padded(source):
        return jnp.concatenate((jnp.zeros((WIN, KVH, DH), source.dtype), source), axis=0)

    def attend_one(inputs):
        part_query, part_key, part_value = inputs
        padded_keys = padded(part_key)
        padded_values = padded(part_value)

        def per_block(block_index):
            block_start = block_index * block_rows
            query_block = lax.dynamic_slice_in_dim(part_query, block_start, block_rows, 0).reshape(1, block_rows, KVH, group_size, DH)
            key_block = lax.dynamic_slice_in_dim(padded_keys, block_start, WIN + block_rows, 0)[None]
            value_block = lax.dynamic_slice_in_dim(padded_values, block_start, WIN + block_rows, 0)[None]
            soft_weights = window_softmax(query_block, key_block, block_start, block_start - WIN)
            mixed = jnp.einsum('sgrtw,swgd->stgrd', soft_weights.astype(jnp.bfloat16), value_block, preferred_element_type=jnp.float32)
            return mixed.reshape(block_rows, MIXER_HEADS, DH)
        blocks_out = lax.map(per_block, jnp.arange(block_count, dtype=jnp.int32))
        return blocks_out.reshape(SEQUENCE_FRAMES, MIXER_HEADS, DH)
    attn_out = lax.map(attend_one, (attn_query, attn_key, attn_value))
    combined = gdn_out + attn_out
    reward = lax.optimization_barrier(jnp.sum(combined * readout.astype(jnp.float32), axis=(2, 3)))
    mask_f = speaker_mask.astype(jnp.float32)
    score = lax.optimization_barrier(jnp.sum(mask_f * reward, axis=1)) * SEQUENCE_FRAMES ** (-0.5)
    pair_index = pair_slot // 2
    role_sign = 1.0 - 2.0 * (pair_slot % 2).astype(jnp.float32)
    member = (pair_index[:, None] == jnp.arange(NPAIRS, dtype=jnp.int32)[None, :]).astype(jnp.float32)
    margins = lax.optimization_barrier(jnp.sum(member * (role_sign * score)[:, None], axis=0)) - ref_margin
    pair_loss = jnp.sum(jax.nn.softplus(-margins)).reshape(1)
    grad_scale = (SEQUENCE_FRAMES * MIXER_HEADS * DH) ** 0.5
    pressure = lax.optimization_barrier(jnp.sum(member * jax.nn.sigmoid(-margins)[None, :], axis=1))
    coefficient = -grad_scale * role_sign * pressure * SEQUENCE_FRAMES ** (-0.5)
    out_grad = coefficient[:, None, None, None] * mask_f[:, :, None, None] * readout.astype(jnp.float32)

    def attend_back(inputs):
        part_query, part_key, part_value, part_grad, part_out = inputs
        padded_keys = padded(part_key)
        padded_values = padded(part_value)

        def per_block(sums, block_index):
            key_sums, value_sums = sums
            block_start = block_index * block_rows
            query_block = lax.dynamic_slice_in_dim(part_query, block_start, block_rows, 0).reshape(1, block_rows, KVH, group_size, DH)
            key_block = lax.dynamic_slice_in_dim(padded_keys, block_start, WIN + block_rows, 0)[None]
            value_block = lax.dynamic_slice_in_dim(padded_values, block_start, WIN + block_rows, 0)[None]
            grad_block = lax.dynamic_slice_in_dim(part_grad, block_start, block_rows, 0).reshape(1, block_rows, KVH, group_size, DH)
            out_block = lax.dynamic_slice_in_dim(part_out, block_start, block_rows, 0).reshape(1, block_rows, KVH, group_size, DH)
            soft_weights = window_softmax(query_block, key_block, block_start, block_start - WIN)
            grad_query, grad_key, grad_value = window_backward(query_block, key_block, value_block, soft_weights, grad_block, out_block)
            key_sums = lax.dynamic_update_slice_in_dim(key_sums, lax.dynamic_slice_in_dim(key_sums, block_start, WIN + block_rows, 0) + grad_key[0], block_start, 0)
            value_sums = lax.dynamic_update_slice_in_dim(value_sums, lax.dynamic_slice_in_dim(value_sums, block_start, WIN + block_rows, 0) + grad_value[0], block_start, 0)
            return ((key_sums, value_sums), grad_query.reshape(block_rows, MIXER_HEADS, DH))
        zero_sums = jnp.zeros((WIN + SEQUENCE_FRAMES, KVH, DH), jnp.float32)
        (key_sums, value_sums), query_blocks = lax.scan(per_block, (zero_sums, zero_sums), jnp.arange(block_count, dtype=jnp.int32))
        return (query_blocks.reshape(SEQUENCE_FRAMES, MIXER_HEADS, DH), key_sums[WIN:], value_sums[WIN:])
    grad_q2, grad_k2, grad_v2 = lax.map(attend_back, (attn_query, attn_key, attn_value, out_grad, attn_out))

    def gdn_back_one(inputs):
        part_query, part_key, part_value, part_decay, part_rate, part_state, part_grad = inputs

        def local_mixer(local_query, local_key, local_value, local_decay, local_rate):
            mixed, final_state = gdn_mixer(local_query[None], local_key[None], local_value[None], local_decay[None], local_rate[None], part_state[None])
            return mixed[0]
        unused_out, pullback = jax.vjp(local_mixer, part_query, part_key, part_value, part_decay, part_rate)
        return pullback(part_grad)
    gq1, gk1, gv1, gdecay, grate = lax.map(gdn_back_one, (query_f, key_f, value_f, log_decay, write_rate, init_state, out_grad))
    return (pair_loss, gq1.astype(jnp.bfloat16), gk1.astype(jnp.bfloat16), gv1.astype(jnp.bfloat16), gdecay, grate, grad_q2.astype(jnp.bfloat16), grad_k2.astype(jnp.bfloat16), grad_v2.astype(jnp.bfloat16))
```

```python
import functools

import jax
import jax.numpy as jnp
from jax import lax
from jax.experimental import pallas as pl
from jax.experimental.pallas import tpu as pltpu
from jax.sharding import PartitionSpec as P

WIN = 512
EPSILON = 1e-06
F32 = jnp.float32
BF16 = jnp.bfloat16
NN = (((1,), (0,)), ((), ()))
NT = (((1,), (1,)), ((), ()))
TN = (((0,), (0,)), ((), ()))


def exact(a, b, dims):
    return lax.dot_general(
        a, b, dims, precision=lax.Precision.HIGHEST, preferred_element_type=F32
    )


def quick(a, b, dims):
    return lax.dot_general(
        a.astype(BF16), b.astype(BF16), dims, preferred_element_type=F32
    )


def parts(a):
    high = a.astype(BF16)
    return high, (a - high.astype(F32)).astype(BF16)


def triple(a, b, dims):
    a_high, a_low = parts(a)
    b_high, b_low = parts(b)
    dot = functools.partial(lax.dot_general, dimension_numbers=dims, preferred_element_type=F32)
    return dot(a_high, b_high) + (dot(a_high, b_low) + dot(a_low, b_high))


INVERT = exact
PREP = exact
RELAY = exact
BACK = exact


def unit_lower_inverse(strict, eye):
    power = [-s for s in strict]
    result = [eye + p for p in power]
    span = 2
    while span < eye.shape[0]:
        power = [INVERT(p, p, NN) for p in power]
        result = [r + INVERT(r, p, NN) for r, p in zip(result, power)]
        span *= 2
    return result


def kernel(
    sizes,
    q_ref,
    k_ref,
    v_ref,
    g_ref,
    b_ref,
    s0_ref,
    aq_ref,
    ak_ref,
    av_ref,
    ro_ref,
    mask_ref,
    slot_ref,
    margin_ref,
    loss_ref,
    dq_ref,
    dk_ref,
    dv_ref,
    dg_ref,
    db_ref,
    daq_ref,
    dak_ref,
    dav_ref,
    window,
    back_send,
    back_recv,
    state_send,
    state_recv,
    grad_send,
    grad_recv,
    score_send,
    score_recv,
    kn_s,
    qn_s,
    map_s,
    shift_s,
    qt_s,
    y0_s,
    p_s,
    l_s,
    m_s,
    a_s,
    w_s,
    u_s,
    z_s,
    col_s,
    state_s,
    next_s,
    local_s,
    g_s,
    b0_s,
    delta_s,
    dq_s,
    aq_grad_s,
    own_s,
    row_s,
    win_send_sem,
    win_recv_sem,
    back_send_sem,
    back_recv_sem,
    state_send_sem,
    state_recv_sem,
    grad_send_sem,
    grad_recv_sem,
    score_send_sem,
    score_recv_sem,
):
    n, pairs, halves = sizes
    group = n * pairs * halves
    pos = lax.axis_index("tm")
    me = (pos * pairs + lax.axis_index("pair")) * halves + lax.axis_index("head")
    frames, heads, width = q_ref.shape[1:]
    blocks = window.shape[0]
    total_frames = frames * n

    def place(index):
        return {
            "tm": index // (pairs * halves),
            "pair": (index // halves) % pairs,
            "head": index % halves,
        }

    barrier = pltpu.get_barrier_semaphore()

    def greet(j, c):
        pl.semaphore_signal(
            barrier,
            inc=1,
            device_id=place(lax.rem(me + j, group)),
            device_id_type=pl.DeviceIdType.MESH,
        )
        return c

    lax.fori_loop(1, group, greet, 0)

    def window_copy(d):
        return pltpu.make_async_remote_copy(
            src_ref=window.at[0],
            dst_ref=window.at[d],
            send_sem=win_send_sem.at[d],
            recv_sem=win_recv_sem.at[d],
            device_id={"tm": pos + d},
            device_id_type=pl.DeviceIdType.MESH,
        )

    def back_copy(d):
        return pltpu.make_async_remote_copy(
            src_ref=back_send.at[d - 1],
            dst_ref=back_recv.at[d - 1],
            send_sem=back_send_sem.at[d],
            recv_sem=back_recv_sem.at[d],
            device_id={"tm": pos - d},
            device_id_type=pl.DeviceIdType.MESH,
        )

    def state_copy(h):
        return pltpu.make_async_remote_copy(
            src_ref=state_send.at[h],
            dst_ref=state_recv.at[h],
            send_sem=state_send_sem.at[h],
            recv_sem=state_recv_sem.at[h],
            device_id={"tm": pos + 1},
            device_id_type=pl.DeviceIdType.MESH,
        )

    def grad_copy(h):
        return pltpu.make_async_remote_copy(
            src_ref=grad_send.at[h],
            dst_ref=grad_recv.at[h],
            send_sem=grad_send_sem.at[h],
            recv_sem=grad_recv_sem.at[h],
            device_id={"tm": pos - 1},
            device_id_type=pl.DeviceIdType.MESH,
        )

    def score_copy(source, target):
        return pltpu.make_async_remote_copy(
            src_ref=score_send,
            dst_ref=score_recv.at[source],
            send_sem=score_send_sem.at[target],
            recv_sem=score_recv_sem.at[source],
            device_id=place(target),
            device_id_type=pl.DeviceIdType.MESH,
        )

    window[0, 0] = ak_ref[0, :, 0, :]
    window[0, 1] = av_ref[0, :, 0, :]
    pl.semaphore_wait(barrier, group - 1)
    for d in range(1, blocks):

        @pl.when(pos + d < n)
        def _():
            window_copy(d).start()

        @pl.when(pos < d)
        def _():
            window[d] = jnp.zeros_like(window[d])

    rows = lax.broadcasted_iota(jnp.int32, (frames, frames), 0)
    cols = lax.broadcasted_iota(jnp.int32, (frames, frames), 1)
    lower = rows >= cols
    strict = rows > cols
    tri = jnp.where(lower, 1.0, 0.0).astype(F32)
    eye = jnp.where(rows == cols, 1.0, 0.0).astype(F32)

    gates = jnp.concatenate([g_ref[0], b_ref[0]], axis=0)
    sum_rows = exact(gates, tri, NT)
    sum_cols = exact(tri, gates, NT)
    gate_cols = exact(eye, gates, NT)
    q_all = q_ref[0].astype(F32)
    k_all = k_ref[0].astype(F32)
    v_all = v_ref[0].astype(F32)
    strict_parts = []
    for h in range(heads):
        kh = k_all[:, h, :]
        qh = q_all[:, h, :]
        rk = lax.rsqrt(jnp.sum(kh * kh, axis=-1, keepdims=True) + EPSILON)
        rq = lax.rsqrt(jnp.sum(qh * qh, axis=-1, keepdims=True) + EPSILON)
        kn = kh * rk
        qn = qh * rq
        kn_s[h] = kn
        qn_s[h] = qn
        col_s[h, :, 0:1] = rk
        col_s[h, :, 1:2] = rq
        c_col = sum_cols[:, h : h + 1]
        c_row = sum_rows[h : h + 1, :]
        beta = gate_cols[:, heads + h : heads + h + 1]
        last = c_col[frames - 1 : frames, :]
        lead = jnp.exp(c_col)
        tail = jnp.exp(last - c_col)
        col_s[h, :, 2:3] = beta
        col_s[h, :, 3:4] = lead
        col_s[h, :, 4:5] = tail
        m = jnp.where(lower, jnp.exp(jnp.where(lower, c_col - c_row, 0.0)), 0.0)
        m_s[h] = m
        both = PREP(jnp.concatenate([kn, qn], axis=0), kn, NT)
        l_mat = jnp.where(strict, beta * m * both[:frames], 0.0)
        l_s[h] = l_mat
        p_s[h] = m * both[frames:]
        strict_parts.append(l_mat)
    inverses = unit_lower_inverse(strict_parts, eye)
    for h in range(heads):
        a = inverses[h]
        a_s[h] = a
        kn = kn_s[h]
        beta = col_s[h, :, 2:3]
        lead = col_s[h, :, 3:4]
        tail = col_s[h, :, 4:5]
        wu = PREP(a, jnp.concatenate([beta * lead * kn, beta * v_all[:, h, :]], axis=1), NN)
        w_s[h] = wu[:, :width]
        u_s[h] = wu[:, width:]
        tk = tail * kn
        ends = PREP(tk, wu, TN)
        map_s[h] = lead[frames - 1 : frames, :] * eye - ends[:, :width]
        shift_s[h] = ends[:, width:]
        inner = PREP(p_s[h], wu, NN)
        qt_s[h] = lead * qn_s[h] - inner[:, :width]
        y0_s[h] = inner[:, width:]
        z_s[h] = PREP(a, tk, TN)

    mask_row = mask_ref[...].astype(F32)
    mask_col = exact(eye, jnp.broadcast_to(mask_row, (8, frames)), NT)[:, 0:1]
    own_s[:, 0:1] = mask_col
    scale = width ** (-0.5)

    def attention():
        for d in range(1, blocks):

            @pl.when(pos >= d)
            def _():
                pltpu.make_async_copy(
                    window.at[d], window.at[d], win_recv_sem.at[d]
                ).wait()

        keys = window[:, 0].reshape(blocks * frames, width)
        values = window[:, 1].reshape(blocks * frames, width)
        t_pos = lax.broadcasted_iota(jnp.int32, (frames, blocks * frames), 0)
        slot = lax.broadcasted_iota(jnp.int32, (frames, blocks * frames), 1)
        distance = slot // frames
        j_pos = slot % frames - distance * frames
        allowed = (j_pos <= t_pos) & (j_pos > t_pos - WIN) & (distance <= pos)
        aq_all = aq_ref[0].astype(F32)
        ro_all = ro_ref[0].astype(F32)
        grad_k = jnp.zeros((blocks * frames, width), F32)
        grad_v = jnp.zeros((blocks * frames, width), F32)
        row_total = jnp.zeros((frames, 1), F32)
        for h in range(heads):
            aq = aq_all[:, h, :].astype(BF16)
            low = (ro_all[:, h, :] * mask_col)
            s = quick(aq, keys, NT) * scale
            s = jnp.where(allowed, s, -jnp.inf)
            e = jnp.exp(s - jnp.max(s, axis=-1, keepdims=True))
            soft = e / jnp.sum(e, axis=-1, keepdims=True)
            weights = soft.astype(BF16)
            out = quick(weights, values, NN)
            row_term = jnp.sum(low * out, axis=-1, keepdims=True)
            row_total = row_total + row_term
            grad_prob = quick(low, values, NT)
            grad_score = (soft * (grad_prob - row_term) * scale).astype(BF16)
            aq_grad_s[h] = quick(grad_score, keys, NN)
            grad_k = grad_k + quick(grad_score, aq, TN)
            grad_v = grad_v + quick(weights, low, TN)
        row_s[...] = jnp.broadcast_to(row_total, row_s.shape)
        own_s[:, width : 2 * width] = grad_k[:frames]
        own_s[:, 2 * width :] = grad_v[:frames]
        for d in range(1, blocks):

            @pl.when(pos >= d)
            def _():
                back_send[d - 1, 0] = grad_k[d * frames : (d + 1) * frames].astype(BF16)
                back_send[d - 1, 1] = grad_v[d * frames : (d + 1) * frames].astype(BF16)
                back_copy(d).start()

    late = pos * 2 >= n
    pl.when(late)(attention)

    for h in range(heads):

        @pl.when(pos == 0)
        def _():
            state_s[h] = s0_ref[0, h]

        @pl.when(pos > 0)
        def _():
            state_copy(h).wait_recv()
            state_s[h] = state_recv[h]

        @pl.when(pos < n - 1)
        def _():
            state_send[h] = shift_s[h] + RELAY(map_s[h], state_s[h], NN)
            state_copy(h).start()

    ro_all = ro_ref[0].astype(F32)
    gdn_rows = jnp.zeros((frames, 1), F32)
    for h in range(heads):
        raw = y0_s[h] + BACK(qt_s[h], state_s[h], NN)
        norm = lax.rsqrt(jnp.mean(raw * raw, axis=-1, keepdims=True) + EPSILON)
        out = raw * norm
        grad = ro_all[:, h, :] * mask_col
        along = jnp.sum(out * grad, axis=-1, keepdims=True)
        gdn_rows = gdn_rows + along
        g_raw = norm * (grad - out * (along * (1.0 / width)))
        g_s[h] = g_raw
        local_s[h] = BACK(qt_s[h], g_raw, TN)

        @pl.when(pos == n - 1)
        def _():
            next_s[h] = jnp.zeros_like(next_s[h])
            grad_send[h] = local_s[h]
            grad_copy(h).start()

    pl.when(jnp.logical_not(late))(attention)

    slot = slot_ref[0]
    sign = 1.0 - 2.0 * (slot % 2).astype(F32)
    tile_pair = lax.broadcasted_iota(jnp.int32, (8, 128), 1)
    member = jnp.where(tile_pair == slot // 2, 1.0, 0.0).astype(F32)
    score = jnp.sum(gdn_rows + row_s[:, 0:1], axis=0, keepdims=True) * total_frames ** (-0.5)
    contribution = member * sign * score
    score_send[...] = contribution
    score_recv[me] = contribution

    def post(j, c):
        score_copy(me, lax.rem(me + j, group)).start()
        return c

    lax.fori_loop(1, group, post, 0)

    for h in range(heads):
        kn = kn_s[h]
        qn = qn_s[h]
        lead = col_s[h, :, 3:4]
        g_raw = g_s[h]
        state = state_s[h]
        delta = u_s[h] - BACK(w_s[h], state, NN)
        delta_s[h] = delta
        b0_s[h] = BACK(a_s[h], BACK(p_s[h], g_raw, TN), TN)
        dp = BACK(g_raw, delta, NT)
        dqk = dp * m_s[h]
        x1 = lead * BACK(g_raw, state, NT)
        dqn = BACK(dqk, kn, NN) + x1
        n_mat = dp * p_s[h]
        local = col_s[h, :, 1:2] * (dqn - qn * jnp.sum(qn * dqn, axis=-1, keepdims=True))
        dq_s[h] = local
        a_s[h] = BACK(dqk, qn, TN)
        p_s[h] = n_mat
        col_s[h, :, 5:6] = jnp.sum(x1 * qn, axis=-1, keepdims=True)

    for h in range(heads):

        @pl.when(pos < n - 1)
        def _():
            grad_copy(h).wait_recv()
            next_s[h] = grad_recv[h]

        @pl.when((pos < n - 1) & (pos > 0))
        def _():
            grad_send[h] = local_s[h] + RELAY(map_s[h], next_s[h], TN)
            grad_copy(h).start()

    def take(j, c):
        score_copy(lax.rem(me + j, group), lax.rem(me + j, group)).wait_recv()
        return c

    lax.fori_loop(1, group, take, 0)
    margin_count = margin_ref.shape[1]
    margin = jnp.sum(score_recv[...], axis=0)[0:1, :margin_count] - margin_ref[...]
    loss = jnp.maximum(-margin, 0.0) + jnp.log1p(jnp.exp(-jnp.abs(margin)))
    loss_ref[...] = jnp.sum(loss, axis=1, keepdims=True)
    pressure = jnp.sum(
        member[0:1, :margin_count] * (1.0 / (1.0 + jnp.exp(margin))), axis=1, keepdims=True
    )
    grad_scale = (total_frames * heads * halves * width) ** 0.5
    coefficient = -grad_scale * sign * pressure * total_frames ** (-0.5)

    dk_list = []
    dv_list = []
    dc_cols = []
    db_cols = []
    n_rows = []
    for h in range(heads):
        kn = kn_s[h]
        rk = col_s[h, :, 0:1]
        beta = col_s[h, :, 2:3]
        lead = col_s[h, :, 3:4]
        tail = col_s[h, :, 4:5]
        later = next_s[h]
        state = state_s[h]
        delta = delta_s[h]
        db = b0_s[h] + BACK(z_s[h], later, NN)
        dl = jnp.where(strict, -BACK(db, delta, NT), 0.0)
        l_term = dl * l_s[h]
        n_mat = p_s[h] + l_term
        dkk = dl * (beta * m_s[h])
        kb = lead * BACK(db, state, NT)
        x2 = -beta * kb
        x3 = tail * BACK(delta, later, NT)
        dkn = a_s[h] + x2 + x3 + BACK(dkk, kn, NN) + BACK(dkk, kn, TN)
        v_h = v_ref[0].astype(F32)[:, h, :]
        dk_list.append(rk * (dkn - kn * jnp.sum(kn * dkn, axis=-1, keepdims=True)))
        dv_list.append(beta * db)
        db_cols.append(
            jnp.sum(db * v_h - kb * kn, axis=-1, keepdims=True)
            + jnp.sum(l_term, axis=-1, keepdims=True) / beta
        )
        tail_term = jnp.sum(x3 * kn, axis=-1, keepdims=True)
        end_term = jnp.sum(tail_term, axis=0, keepdims=True) + lead[
            frames - 1 : frames, :
        ] * jnp.sum(jnp.sum(later * state, axis=-1, keepdims=True), axis=0, keepdims=True)
        dc = (
            jnp.sum(n_mat, axis=-1, keepdims=True)
            + col_s[h, :, 5:6]
            + jnp.sum(x2 * kn, axis=-1, keepdims=True)
            - tail_term
        )
        dc = dc + jnp.where(rows[:, 0:1] == frames - 1, end_term, 0.0)
        dc_cols.append(dc)
        n_rows.append(jnp.sum(n_mat, axis=0, keepdims=True))
    cols_all = jnp.concatenate(dc_cols + db_cols, axis=1)
    pad = [jnp.zeros((heads, frames), F32)]
    n_all = jnp.concatenate(n_rows + pad, axis=0)
    dg = (exact(cols_all, tri, TN) - exact(n_all, tri, NN))[:heads]
    dbeta = exact(cols_all, eye, TN)[heads:]
    dg_ref[0] = coefficient * dg
    db_ref[0] = coefficient * dbeta
    dq_ref[0] = jnp.stack([dq_s[h] * coefficient for h in range(heads)], axis=1).astype(BF16)
    dk_ref[0] = jnp.stack([x * coefficient for x in dk_list], axis=1).astype(BF16)
    dv_ref[0] = jnp.stack([x * coefficient for x in dv_list], axis=1).astype(BF16)
    daq_ref[0] = jnp.stack(
        [aq_grad_s[h] * coefficient for h in range(heads)], axis=1
    ).astype(BF16)

    for d in range(1, blocks):

        @pl.when(pos + d < n)
        def _():
            pltpu.make_async_copy(
                back_recv.at[d - 1], back_recv.at[d - 1], back_recv_sem.at[d]
            ).wait()
            own_s[:, width : 2 * width] += back_recv[d - 1, 0].astype(F32)
            own_s[:, 2 * width :] += back_recv[d - 1, 1].astype(F32)

    dak_ref[0] = (own_s[:, width : 2 * width] * coefficient).astype(BF16)[:, None, :]
    dav_ref[0] = (own_s[:, 2 * width :] * coefficient).astype(BF16)[:, None, :]

    for d in range(1, blocks):

        @pl.when(pos + d < n)
        def _():
            window_copy(d).wait_send()

        @pl.when(pos >= d)
        def _():
            back_copy(d).wait_send()

    for h in range(heads):

        @pl.when(pos < n - 1)
        def _():
            state_copy(h).wait_send()

        @pl.when(pos > 0)
        def _():
            grad_copy(h).wait_send()

    def sent(j, c):
        score_copy(me, lax.rem(me + j, group)).wait_send()
        return c

    lax.fori_loop(1, group, sent, 0)


def body(
    sizes,
    gdn_query,
    gdn_key,
    gdn_value,
    log_decay,
    write_rate,
    init_state,
    attn_query,
    attn_key,
    attn_value,
    readout,
    speaker_mask,
    pair_slot,
    ref_margin,
):
    n, pairs, halves = sizes
    group = n * pairs * halves
    seq, frames, heads, width = gdn_query.shape
    blocks = min(WIN // frames, n - 1) + 1
    vmem = pl.BlockSpec(memory_space=pltpu.VMEM)
    smem = pl.BlockSpec(memory_space=pltpu.SMEM)
    dma = pltpu.SemaphoreType.DMA
    square = pltpu.VMEM((heads, frames, width), F32)
    state_square = pltpu.VMEM((heads, width, width), F32)
    shape = jax.ShapeDtypeStruct
    out = pl.pallas_call(
        functools.partial(kernel, sizes),
        out_shape=(
            shape((1, 1), F32),
            shape(gdn_query.shape, BF16),
            shape(gdn_key.shape, BF16),
            shape(gdn_value.shape, BF16),
            shape(log_decay.shape, F32),
            shape(write_rate.shape, F32),
            shape(attn_query.shape, BF16),
            shape(attn_key.shape, BF16),
            shape(attn_value.shape, BF16),
        ),
        in_specs=[vmem] * 11 + [smem, vmem],
        out_specs=(vmem,) * 9,
        scratch_shapes=[
            pltpu.VMEM((blocks, 2, frames, width), BF16),
            pltpu.VMEM((blocks - 1, 2, frames, width), BF16),
            pltpu.VMEM((blocks - 1, 2, frames, width), BF16),
            state_square,
            state_square,
            state_square,
            state_square,
            pltpu.VMEM((8, 128), F32),
            pltpu.VMEM((group, 8, 128), F32),
        ]
        + [square] * 13
        + [pltpu.VMEM((heads, frames, 128), F32)]
        + [square] * 8
        + [pltpu.VMEM((frames, 3 * width), F32), pltpu.VMEM((frames, 128), F32)]
        + [
            dma((blocks,)),
            dma((blocks,)),
            dma((blocks,)),
            dma((blocks,)),
            dma((heads,)),
            dma((heads,)),
            dma((heads,)),
            dma((heads,)),
            dma((group,)),
            dma((group,)),
        ],
        compiler_params=pltpu.CompilerParams(
            collective_id=0, has_side_effects=True, vmem_limit_bytes=40 * 1024 * 1024
        ),
    )(
        gdn_query,
        gdn_key,
        gdn_value,
        log_decay,
        write_rate,
        init_state,
        attn_query,
        attn_key,
        attn_value,
        readout,
        speaker_mask,
        pair_slot,
        ref_margin.reshape(1, -1),
    )
    return (out[0].reshape(1),) + tuple(out[1:])


def solution(mesh):
    sizes = (mesh.shape["tm"], mesh.shape["pair"], mesh.shape["head"])
    wide = P(("groups", "pair"), "tm", "head", None)
    gate = P(("groups", "pair"), "head", "tm")
    return jax.shard_map(
        functools.partial(body, sizes),
        mesh=mesh,
        in_specs=(
            wide,
            wide,
            wide,
            gate,
            gate,
            P(("groups", "pair"), "head", None, None),
            wide,
            wide,
            wide,
            wide,
            P(("groups", "pair"), "tm"),
            P(("groups", "pair")),
            P("groups"),
        ),
        out_specs=(P("groups"), wide, wide, wide, gate, gate, wide, wide, wide),
        check_vma=False,
    )
```

```python
import functools

import jax
import jax.numpy as jnp
from jax import lax
from jax.experimental import pallas as pl
from jax.experimental.pallas import tpu as pltpu
from jax.sharding import PartitionSpec as P

WIN = 512
EPSILON = 1e-06
F32 = jnp.float32
BF16 = jnp.bfloat16
NN = (((1,), (0,)), ((), ()))
NT = (((1,), (1,)), ((), ()))
TN = (((0,), (0,)), ((), ()))


def exact(a, b, dims):
    return lax.dot_general(
        a, b, dims, precision=lax.Precision.HIGHEST, preferred_element_type=F32
    )


def quick(a, b, dims):
    return lax.dot_general(
        a.astype(BF16), b.astype(BF16), dims, preferred_element_type=F32
    )


def parts(a):
    high = a.astype(BF16)
    return high, (a - high.astype(F32)).astype(BF16)


def triple(a, b, dims):
    a_high, a_low = parts(a)
    b_high, b_low = parts(b)
    dot = functools.partial(lax.dot_general, dimension_numbers=dims, preferred_element_type=F32)
    return dot(a_high, b_high) + (dot(a_high, b_low) + dot(a_low, b_high))


INVERT = triple
PREP = triple
RELAY = triple
BACK = triple


def unit_lower_inverse(strict, eye):
    power = [-s for s in strict]
    result = [eye + p for p in power]
    span = 2
    while span < eye.shape[0]:
        power = [INVERT(p, p, NN) for p in power]
        result = [r + INVERT(r, p, NN) for r, p in zip(result, power)]
        span *= 2
    return result


def kernel(
    sizes,
    fetches,
    q_ref,
    k_ref,
    v_ref,
    g_ref,
    b_ref,
    s0_ref,
    aq_ref,
    ro_ref,
    mask_ref,
    slot_ref,
    margin_ref,
    loss_ref,
    dq_ref,
    dk_ref,
    dv_ref,
    dg_ref,
    db_ref,
    daq_ref,
    dak_ref,
    dav_ref,
    window,
    back_send,
    back_recv,
    state_send,
    state_recv,
    grad_send,
    grad_recv,
    score_send,
    score_recv,
    kn_s,
    qn_s,
    map_s,
    shift_s,
    qt_s,
    y0_s,
    p_s,
    l_s,
    m_s,
    a_s,
    w_s,
    u_s,
    z_s,
    col_s,
    state_s,
    next_s,
    local_s,
    g_s,
    b0_s,
    delta_s,
    dq_s,
    aq_grad_s,
    own_s,
    row_s,
    win_send_sem,
    win_recv_sem,
    back_send_sem,
    back_recv_sem,
    state_send_sem,
    state_recv_sem,
    grad_send_sem,
    grad_recv_sem,
    score_send_sem,
    score_recv_sem,
):
    n, pairs, halves = sizes
    group = n * pairs * halves
    pos = lax.axis_index("tm")
    me = (pos * pairs + lax.axis_index("pair")) * halves + lax.axis_index("head")
    frames, heads, width = q_ref.shape[1:]
    blocks = window.shape[0]
    total_frames = frames * n

    def place(index):
        return {
            "tm": index // (pairs * halves),
            "pair": (index // halves) % pairs,
            "head": index % halves,
        }

    barrier = pltpu.get_barrier_semaphore()

    def greet(j, c):
        pl.semaphore_signal(
            barrier,
            inc=1,
            device_id=place(lax.rem(me + j, group)),
            device_id_type=pl.DeviceIdType.MESH,
        )
        return c

    lax.fori_loop(1, group, greet, 0)

    def window_copy(d):
        return pltpu.make_async_remote_copy(
            src_ref=window.at[0],
            dst_ref=window.at[d],
            send_sem=win_send_sem.at[d],
            recv_sem=win_recv_sem.at[d],
            device_id={"tm": pos + d},
            device_id_type=pl.DeviceIdType.MESH,
        )

    def back_copy(d):
        return pltpu.make_async_remote_copy(
            src_ref=back_send.at[d - 1],
            dst_ref=back_recv.at[d - 1],
            send_sem=back_send_sem.at[d],
            recv_sem=back_recv_sem.at[d],
            device_id={"tm": pos - d},
            device_id_type=pl.DeviceIdType.MESH,
        )

    def state_copy(h):
        return pltpu.make_async_remote_copy(
            src_ref=state_send.at[h],
            dst_ref=state_recv.at[h],
            send_sem=state_send_sem.at[h],
            recv_sem=state_recv_sem.at[h],
            device_id={"tm": pos + 1},
            device_id_type=pl.DeviceIdType.MESH,
        )

    def grad_copy(h):
        return pltpu.make_async_remote_copy(
            src_ref=grad_send.at[h],
            dst_ref=grad_recv.at[h],
            send_sem=grad_send_sem.at[h],
            recv_sem=grad_recv_sem.at[h],
            device_id={"tm": pos - 1},
            device_id_type=pl.DeviceIdType.MESH,
        )

    def score_copy(source, target):
        return pltpu.make_async_remote_copy(
            src_ref=score_send,
            dst_ref=score_recv.at[source],
            send_sem=score_send_sem.at[target],
            recv_sem=score_recv_sem.at[source],
            device_id=place(target),
            device_id_type=pl.DeviceIdType.MESH,
        )

    fetches[7].wait()
    fetches[8].wait()
    pl.semaphore_wait(barrier, group - 1)
    for d in range(1, blocks):

        @pl.when(pos + d < n)
        def _():
            window_copy(d).start()

        @pl.when(pos < d)
        def _():
            window[d] = jnp.zeros_like(window[d])

    rows = lax.broadcasted_iota(jnp.int32, (frames, frames), 0)
    cols = lax.broadcasted_iota(jnp.int32, (frames, frames), 1)
    lower = rows >= cols
    strict = rows > cols
    tri = jnp.where(lower, 1.0, 0.0).astype(F32)
    eye = jnp.where(rows == cols, 1.0, 0.0).astype(F32)

    for i in (3, 4, 1, 0, 2, 10, 5, 6, 9):
        fetches[i].wait()
    gates = jnp.concatenate([g_ref[0], b_ref[0]], axis=0)
    sum_rows = exact(gates, tri, NT)
    sum_cols = exact(tri, gates, NT)
    gate_cols = exact(eye, gates, NT)
    q_all = q_ref[0].astype(F32)
    k_all = k_ref[0].astype(F32)
    v_all = v_ref[0].astype(F32)
    strict_parts = []
    for h in range(heads):
        kh = k_all[:, h, :]
        qh = q_all[:, h, :]
        rk = lax.rsqrt(jnp.sum(kh * kh, axis=-1, keepdims=True) + EPSILON)
        rq = lax.rsqrt(jnp.sum(qh * qh, axis=-1, keepdims=True) + EPSILON)
        kn = kh * rk
        qn = qh * rq
        kn_s[h] = kn
        qn_s[h] = qn
        col_s[h, :, 0:1] = rk
        col_s[h, :, 1:2] = rq
        c_col = sum_cols[:, h : h + 1]
        c_row = sum_rows[h : h + 1, :]
        beta = gate_cols[:, heads + h : heads + h + 1]
        last = c_col[frames - 1 : frames, :]
        lead = jnp.exp(c_col)
        tail = jnp.exp(last - c_col)
        col_s[h, :, 2:3] = beta
        col_s[h, :, 3:4] = lead
        col_s[h, :, 4:5] = tail
        m = jnp.where(lower, jnp.exp(jnp.where(lower, c_col - c_row, 0.0)), 0.0)
        m_s[h] = m
        both = PREP(jnp.concatenate([kn, qn], axis=0), kn, NT)
        l_mat = jnp.where(strict, beta * m * both[:frames], 0.0)
        l_s[h] = l_mat
        p_s[h] = m * both[frames:]
        strict_parts.append(l_mat)
    inverses = unit_lower_inverse(strict_parts, eye)
    for h in range(heads):
        a = inverses[h]
        a_s[h] = a
        kn = kn_s[h]
        beta = col_s[h, :, 2:3]
        lead = col_s[h, :, 3:4]
        tail = col_s[h, :, 4:5]
        wu = PREP(a, jnp.concatenate([beta * lead * kn, beta * v_all[:, h, :]], axis=1), NN)
        w_s[h] = wu[:, :width]
        u_s[h] = wu[:, width:]
        tk = tail * kn
        ends = PREP(tk, wu, TN)
        map_s[h] = lead[frames - 1 : frames, :] * eye - ends[:, :width]
        shift_s[h] = ends[:, width:]
        inner = PREP(p_s[h], wu, NN)
        qt_s[h] = lead * qn_s[h] - inner[:, :width]
        y0_s[h] = inner[:, width:]
        z_s[h] = PREP(a, tk, TN)

    mask_row = mask_ref[...].astype(F32)
    mask_col = exact(eye, jnp.broadcast_to(mask_row, (8, frames)), NT)[:, 0:1]
    own_s[:, 0:1] = mask_col
    scale = width ** (-0.5)

    def attention():
        for d in range(1, blocks):

            @pl.when(pos >= d)
            def _():
                pltpu.make_async_copy(
                    window.at[d], window.at[d], win_recv_sem.at[d]
                ).wait()

        keys = window[:, 0].reshape(blocks * frames, width)
        values = window[:, 1].reshape(blocks * frames, width)
        t_pos = lax.broadcasted_iota(jnp.int32, (frames, blocks * frames), 0)
        slot = lax.broadcasted_iota(jnp.int32, (frames, blocks * frames), 1)
        distance = slot // frames
        j_pos = slot % frames - distance * frames
        allowed = (j_pos <= t_pos) & (j_pos > t_pos - WIN) & (distance <= pos)
        aq_all = aq_ref[0].astype(F32)
        ro_all = ro_ref[0].astype(F32)
        grad_k = jnp.zeros((blocks * frames, width), F32)
        grad_v = jnp.zeros((blocks * frames, width), F32)
        row_total = jnp.zeros((frames, 1), F32)
        for h in range(heads):
            aq = aq_all[:, h, :].astype(BF16)
            low = (ro_all[:, h, :] * mask_col)
            s = quick(aq, keys, NT) * scale
            s = jnp.where(allowed, s, -jnp.inf)
            e = jnp.exp(s - jnp.max(s, axis=-1, keepdims=True))
            soft = e / jnp.sum(e, axis=-1, keepdims=True)
            weights = soft.astype(BF16)
            out = quick(weights, values, NN)
            row_term = jnp.sum(low * out, axis=-1, keepdims=True)
            row_total = row_total + row_term
            grad_prob = quick(low, values, NT)
            grad_score = (soft * (grad_prob - row_term) * scale).astype(BF16)
            aq_grad_s[h] = quick(grad_score, keys, NN)
            grad_k = grad_k + quick(grad_score, aq, TN)
            grad_v = grad_v + quick(weights, low, TN)
        row_s[...] = jnp.broadcast_to(row_total, row_s.shape)
        own_s[:, width : 2 * width] = grad_k[:frames]
        own_s[:, 2 * width :] = grad_v[:frames]
        for d in range(1, blocks):

            @pl.when(pos >= d)
            def _():
                back_send[d - 1, 0] = grad_k[d * frames : (d + 1) * frames].astype(BF16)
                back_send[d - 1, 1] = grad_v[d * frames : (d + 1) * frames].astype(BF16)
                back_copy(d).start()

    late = pos * 2 >= n
    pl.when(late)(attention)

    for h in range(heads):

        @pl.when(pos == 0)
        def _():
            state_s[h] = s0_ref[0, h]

        @pl.when(pos > 0)
        def _():
            state_copy(h).wait_recv()
            state_s[h] = state_recv[h]

        @pl.when(pos < n - 1)
        def _():
            state_send[h] = shift_s[h] + RELAY(map_s[h], state_s[h], NN)
            state_copy(h).start()

    ro_all = ro_ref[0].astype(F32)
    gdn_rows = jnp.zeros((frames, 1), F32)
    for h in range(heads):
        raw = y0_s[h] + BACK(qt_s[h], state_s[h], NN)
        norm = lax.rsqrt(jnp.mean(raw * raw, axis=-1, keepdims=True) + EPSILON)
        out = raw * norm
        grad = ro_all[:, h, :] * mask_col
        along = jnp.sum(out * grad, axis=-1, keepdims=True)
        gdn_rows = gdn_rows + along
        g_raw = norm * (grad - out * (along * (1.0 / width)))
        g_s[h] = g_raw
        local_s[h] = BACK(qt_s[h], g_raw, TN)

        @pl.when(pos == n - 1)
        def _():
            next_s[h] = jnp.zeros_like(next_s[h])
            grad_send[h] = local_s[h]
            grad_copy(h).start()

    pl.when(jnp.logical_not(late))(attention)

    slot = slot_ref[0]
    sign = 1.0 - 2.0 * (slot % 2).astype(F32)
    tile_pair = lax.broadcasted_iota(jnp.int32, (8, 128), 1)
    member = jnp.where(tile_pair == slot // 2, 1.0, 0.0).astype(F32)
    score = jnp.sum(gdn_rows + row_s[:, 0:1], axis=0, keepdims=True) * total_frames ** (-0.5)
    contribution = member * sign * score
    score_send[...] = contribution
    score_recv[me] = contribution

    def post(j, c):
        score_copy(me, lax.rem(me + j, group)).start()
        return c

    lax.fori_loop(1, group, post, 0)

    for h in range(heads):
        kn = kn_s[h]
        qn = qn_s[h]
        lead = col_s[h, :, 3:4]
        g_raw = g_s[h]
        state = state_s[h]
        delta = u_s[h] - BACK(w_s[h], state, NN)
        delta_s[h] = delta
        b0_s[h] = BACK(a_s[h], BACK(p_s[h], g_raw, TN), TN)
        dp = BACK(g_raw, delta, NT)
        dqk = dp * m_s[h]
        x1 = lead * BACK(g_raw, state, NT)
        dqn = quick(dqk, kn, NN) + x1
        n_mat = dp * p_s[h]
        local = col_s[h, :, 1:2] * (dqn - qn * jnp.sum(qn * dqn, axis=-1, keepdims=True))
        dq_s[h] = local
        a_s[h] = quick(dqk, qn, TN)
        p_s[h] = n_mat
        col_s[h, :, 5:6] = jnp.sum(x1 * qn, axis=-1, keepdims=True)

    for h in range(heads):

        @pl.when(pos < n - 1)
        def _():
            grad_copy(h).wait_recv()
            next_s[h] = grad_recv[h]

        @pl.when((pos < n - 1) & (pos > 0))
        def _():
            grad_send[h] = local_s[h] + RELAY(map_s[h], next_s[h], TN)
            grad_copy(h).start()

    def take(j, c):
        score_copy(lax.rem(me + j, group), lax.rem(me + j, group)).wait_recv()
        return c

    lax.fori_loop(1, group, take, 0)
    margin_count = margin_ref.shape[1]
    margin = jnp.sum(score_recv[...], axis=0)[0:1, :margin_count] - margin_ref[...]
    loss = jnp.maximum(-margin, 0.0) + jnp.log1p(jnp.exp(-jnp.abs(margin)))
    loss_ref[...] = jnp.sum(loss, axis=1, keepdims=True)
    pressure = jnp.sum(
        member[0:1, :margin_count] * (1.0 / (1.0 + jnp.exp(margin))), axis=1, keepdims=True
    )
    grad_scale = (total_frames * heads * halves * width) ** 0.5
    coefficient = -grad_scale * sign * pressure * total_frames ** (-0.5)

    dk_list = []
    dv_list = []
    dc_cols = []
    db_cols = []
    n_rows = []
    for h in range(heads):
        kn = kn_s[h]
        rk = col_s[h, :, 0:1]
        beta = col_s[h, :, 2:3]
        lead = col_s[h, :, 3:4]
        tail = col_s[h, :, 4:5]
        later = next_s[h]
        state = state_s[h]
        delta = delta_s[h]
        db = b0_s[h] + BACK(z_s[h], later, NN)
        dl = jnp.where(strict, -BACK(db, delta, NT), 0.0)
        l_term = dl * l_s[h]
        n_mat = p_s[h] + l_term
        dkk = dl * (beta * m_s[h])
        kb = lead * BACK(db, state, NT)
        x2 = -beta * kb
        x3 = tail * BACK(delta, later, NT)
        dkn = a_s[h] + x2 + x3 + quick(dkk, kn, NN) + quick(dkk, kn, TN)
        v_h = v_ref[0].astype(F32)[:, h, :]
        dk_list.append(rk * (dkn - kn * jnp.sum(kn * dkn, axis=-1, keepdims=True)))
        dv_list.append(beta * db)
        db_cols.append(
            jnp.sum(db * v_h - kb * kn, axis=-1, keepdims=True)
            + jnp.sum(l_term, axis=-1, keepdims=True) / beta
        )
        tail_term = jnp.sum(x3 * kn, axis=-1, keepdims=True)
        end_term = jnp.sum(tail_term, axis=0, keepdims=True) + lead[
            frames - 1 : frames, :
        ] * jnp.sum(jnp.sum(later * state, axis=-1, keepdims=True), axis=0, keepdims=True)
        dc = (
            jnp.sum(n_mat, axis=-1, keepdims=True)
            + col_s[h, :, 5:6]
            + jnp.sum(x2 * kn, axis=-1, keepdims=True)
            - tail_term
        )
        dc = dc + jnp.where(rows[:, 0:1] == frames - 1, end_term, 0.0)
        dc_cols.append(dc)
        n_rows.append(jnp.sum(n_mat, axis=0, keepdims=True))
    cols_all = jnp.concatenate(dc_cols + db_cols, axis=1)
    pad = [jnp.zeros((heads, frames), F32)]
    n_all = jnp.concatenate(n_rows + pad, axis=0)
    dg = (exact(cols_all, tri, TN) - exact(n_all, tri, NN))[:heads]
    dbeta = exact(cols_all, eye, TN)[heads:]
    dg_ref[0] = coefficient * dg
    db_ref[0] = coefficient * dbeta
    dq_ref[0] = jnp.stack([dq_s[h] * coefficient for h in range(heads)], axis=1).astype(BF16)
    dk_ref[0] = jnp.stack([x * coefficient for x in dk_list], axis=1).astype(BF16)
    dv_ref[0] = jnp.stack([x * coefficient for x in dv_list], axis=1).astype(BF16)
    daq_ref[0] = jnp.stack(
        [aq_grad_s[h] * coefficient for h in range(heads)], axis=1
    ).astype(BF16)

    for d in range(1, blocks):

        @pl.when(pos + d < n)
        def _():
            pltpu.make_async_copy(
                back_recv.at[d - 1], back_recv.at[d - 1], back_recv_sem.at[d]
            ).wait()
            own_s[:, width : 2 * width] += back_recv[d - 1, 0].astype(F32)
            own_s[:, 2 * width :] += back_recv[d - 1, 1].astype(F32)

    dak_ref[...] = (own_s[:, width : 2 * width] * coefficient).astype(BF16)
    dav_ref[...] = (own_s[:, 2 * width :] * coefficient).astype(BF16)

    for d in range(1, blocks):

        @pl.when(pos + d < n)
        def _():
            window_copy(d).wait_send()

        @pl.when(pos >= d)
        def _():
            back_copy(d).wait_send()

    for h in range(heads):

        @pl.when(pos < n - 1)
        def _():
            state_copy(h).wait_send()

        @pl.when(pos > 0)
        def _():
            grad_copy(h).wait_send()

    def sent(j, c):
        score_copy(me, lax.rem(me + j, group)).wait_send()
        return c

    lax.fori_loop(1, group, sent, 0)


def entry(sizes, *refs):
    sources, small = refs[:11], refs[11:13]
    results, rest = refs[13:22], refs[22:]
    held, fetch_sem, scratch = rest[:9], rest[9], rest[10:]
    window = scratch[0]
    targets = list(held[:7]) + [window.at[0, 0], window.at[0, 1]] + list(held[7:])
    copies = [
        pltpu.make_async_copy(source, target, fetch_sem.at[i])
        for i, (source, target) in enumerate(zip(sources, targets))
    ]
    for i in FETCH_ORDER:
        copies[i].start()
    kernel(sizes, copies, *held, *small, *results, *scratch)


def hand_over(*refs):
    count = (len(refs) - 1) // 2
    copies = [
        pltpu.make_async_copy(refs[i], refs[count + i], refs[-1].at[i]) for i in range(count)
    ]
    for copy in copies:
        copy.start()
    for copy in copies:
        copy.wait()


FETCH_ORDER = (7, 8, 3, 4, 1, 0, 2, 10, 5, 6, 9)


def body(
    sizes,
    gdn_query,
    gdn_key,
    gdn_value,
    log_decay,
    write_rate,
    init_state,
    attn_query,
    attn_key,
    attn_value,
    readout,
    speaker_mask,
    pair_slot,
    ref_margin,
):
    n, pairs, halves = sizes
    group = n * pairs * halves
    seq, frames, heads, width = gdn_query.shape
    blocks = min(WIN // frames, n - 1) + 1
    vmem = pl.BlockSpec(memory_space=pltpu.VMEM)
    hbm = pl.BlockSpec(memory_space=pltpu.HBM)
    smem = pl.BlockSpec(memory_space=pltpu.SMEM)
    dma = pltpu.SemaphoreType.DMA
    square = pltpu.VMEM((heads, frames, width), F32)
    state_square = pltpu.VMEM((heads, width, width), F32)
    shape = jax.ShapeDtypeStruct
    out = pl.pallas_call(
        functools.partial(entry, sizes),
        out_shape=(
            shape((1, 1), F32),
            shape(gdn_query.shape, BF16),
            shape(gdn_key.shape, BF16),
            shape(gdn_value.shape, BF16),
            shape(log_decay.shape, F32),
            shape(write_rate.shape, F32),
            shape(attn_query.shape, BF16),
            shape((frames, width), BF16),
            shape((frames, width), BF16),
        ),
        in_specs=[hbm] * 11 + [smem, vmem],
        out_specs=(vmem,) * 9,
        scratch_shapes=[pltpu.VMEM(gdn_query.shape, BF16)] * 3
        + [pltpu.VMEM(log_decay.shape, F32)] * 2
        + [
            pltpu.VMEM(init_state.shape, F32),
            pltpu.VMEM(attn_query.shape, BF16),
            pltpu.VMEM(readout.shape, BF16),
            pltpu.VMEM(speaker_mask.shape, jnp.int32),
            dma((11,)),
            pltpu.VMEM((blocks, 2, frames, width), BF16),
            pltpu.VMEM((blocks - 1, 2, frames, width), BF16),
            pltpu.VMEM((blocks - 1, 2, frames, width), BF16),
            state_square,
            state_square,
            state_square,
            state_square,
            pltpu.VMEM((8, 128), F32),
            pltpu.VMEM((group, 8, 128), F32),
        ]
        + [square] * 13
        + [pltpu.VMEM((heads, frames, 128), F32)]
        + [square] * 8
        + [pltpu.VMEM((frames, 3 * width), F32), pltpu.VMEM((frames, 128), F32)]
        + [
            dma((blocks,)),
            dma((blocks,)),
            dma((blocks,)),
            dma((blocks,)),
            dma((heads,)),
            dma((heads,)),
            dma((heads,)),
            dma((heads,)),
            dma((group,)),
            dma((group,)),
        ],
        compiler_params=pltpu.CompilerParams(
            collective_id=0, has_side_effects=True, vmem_limit_bytes=62 * 1024 * 1024
        ),
    )(
        gdn_query,
        gdn_key,
        gdn_value,
        log_decay,
        write_rate,
        init_state,
        attn_query,
        attn_key.reshape(frames, width),
        attn_value.reshape(frames, width),
        readout,
        speaker_mask,
        pair_slot,
        ref_margin.reshape(1, -1),
    )
    final = pl.pallas_call(
        hand_over,
        out_shape=tuple(shape(a.shape, a.dtype) for a in out[1:]),
        in_specs=[hbm] * 8,
        out_specs=(hbm,) * 8,
        scratch_shapes=[dma((8,))],
        compiler_params=pltpu.CompilerParams(vmem_limit_bytes=62 * 1024 * 1024),
    )(*out[1:])
    return (
        (out[0].reshape(1),)
        + tuple(final[:6])
        + (final[6].reshape(attn_key.shape), final[7].reshape(attn_value.shape))
    )


def solution(mesh):
    sizes = (mesh.shape["tm"], mesh.shape["pair"], mesh.shape["head"])
    wide = P(("groups", "pair"), "tm", "head", None)
    gate = P(("groups", "pair"), "head", "tm")
    return jax.shard_map(
        functools.partial(body, sizes),
        mesh=mesh,
        in_specs=(
            wide,
            wide,
            wide,
            gate,
            gate,
            P(("groups", "pair"), "head", None, None),
            wide,
            wide,
            wide,
            wide,
            P(("groups", "pair"), "tm"),
            P(("groups", "pair")),
            P("groups"),
        ),
        out_specs=(P("groups"), wide, wide, wide, gate, gate, wide, wide, wide),
        check_vma=False,
    )
```

```python
import functools

import jax
import jax.numpy as jnp
from jax import lax
from jax.experimental import pallas as pl
from jax.experimental.pallas import tpu as pltpu
from jax.sharding import PartitionSpec as P

WIN = 512
EPSILON = 1e-06
F32 = jnp.float32
BF16 = jnp.bfloat16
NN = (((1,), (0,)), ((), ()))
NT = (((1,), (1,)), ((), ()))
TN = (((0,), (0,)), ((), ()))


def exact(a, b, dims):
    return lax.dot_general(
        a, b, dims, precision=lax.Precision.HIGHEST, preferred_element_type=F32
    )


def quick(a, b, dims):
    return lax.dot_general(
        a.astype(BF16), b.astype(BF16), dims, preferred_element_type=F32
    )


def parts(a):
    high = a.astype(BF16)
    return high, (a - high.astype(F32)).astype(BF16)


def triple(a, b, dims):
    a_high, a_low = parts(a)
    b_high, b_low = parts(b)
    dot = functools.partial(lax.dot_general, dimension_numbers=dims, preferred_element_type=F32)
    return dot(a_high, b_high) + (dot(a_high, b_low) + dot(a_low, b_high))


INVERT = triple
PREP = triple
RELAY = triple
BACK = triple


def unit_lower_inverse(strict, eye):
    power = [-s for s in strict]
    result = [eye + p for p in power]
    span = 2
    while span < eye.shape[0]:
        power = [INVERT(p, p, NN) for p in power]
        result = [r + INVERT(r, p, NN) for r, p in zip(result, power)]
        span *= 2
    return result


def kernel(
    sizes,
    fetches,
    q_ref,
    k_ref,
    v_ref,
    g_ref,
    b_ref,
    s0_ref,
    aq_ref,
    ro_ref,
    mask_ref,
    slot_ref,
    margin_ref,
    loss_ref,
    dq_ref,
    dk_ref,
    dv_ref,
    dg_ref,
    db_ref,
    daq_ref,
    dak_ref,
    dav_ref,
    window,
    back_send,
    back_recv,
    state_send,
    state_recv,
    grad_send,
    grad_recv,
    score_send,
    score_recv,
    kn_s,
    qn_s,
    map_s,
    map_t_s,
    shift_s,
    qt_s,
    y0_s,
    p_s,
    l_s,
    m_s,
    a_s,
    w_s,
    u_s,
    z_s,
    col_s,
    state_s,
    next_s,
    local_s,
    g_s,
    b0_s,
    delta_s,
    dq_s,
    aq_grad_s,
    own_s,
    row_s,
    win_send_sem,
    win_recv_sem,
    back_send_sem,
    back_recv_sem,
    state_send_sem,
    state_recv_sem,
    grad_send_sem,
    grad_recv_sem,
    score_send_sem,
    score_recv_sem,
):
    n, pairs, halves = sizes
    group = n * pairs * halves
    pos = lax.axis_index("tm")
    me = (pos * pairs + lax.axis_index("pair")) * halves + lax.axis_index("head")
    frames, heads, width = q_ref.shape[1:]
    blocks = window.shape[0]
    total_frames = frames * n

    def place(index):
        return {
            "tm": index // (pairs * halves),
            "pair": (index // halves) % pairs,
            "head": index % halves,
        }

    barrier = pltpu.get_barrier_semaphore()

    def greet(j, c):
        pl.semaphore_signal(
            barrier,
            inc=1,
            device_id=place(lax.rem(me + j, group)),
            device_id_type=pl.DeviceIdType.MESH,
        )
        return c

    lax.fori_loop(1, group, greet, 0)

    def window_copy(d):
        return pltpu.make_async_remote_copy(
            src_ref=window.at[0],
            dst_ref=window.at[d],
            send_sem=win_send_sem.at[d],
            recv_sem=win_recv_sem.at[d],
            device_id={"tm": pos + d},
            device_id_type=pl.DeviceIdType.MESH,
        )

    def back_copy(d):
        return pltpu.make_async_remote_copy(
            src_ref=back_send.at[d - 1],
            dst_ref=back_recv.at[d - 1],
            send_sem=back_send_sem.at[d],
            recv_sem=back_recv_sem.at[d],
            device_id={"tm": pos - d},
            device_id_type=pl.DeviceIdType.MESH,
        )

    def state_copy(h):
        return pltpu.make_async_remote_copy(
            src_ref=state_send.at[h],
            dst_ref=state_recv.at[h],
            send_sem=state_send_sem.at[h],
            recv_sem=state_recv_sem.at[h],
            device_id={"tm": pos + 1},
            device_id_type=pl.DeviceIdType.MESH,
        )

    def grad_copy(h):
        return pltpu.make_async_remote_copy(
            src_ref=grad_send.at[h],
            dst_ref=grad_recv.at[h],
            send_sem=grad_send_sem.at[h],
            recv_sem=grad_recv_sem.at[h],
            device_id={"tm": pos - 1},
            device_id_type=pl.DeviceIdType.MESH,
        )

    def score_copy(source, target):
        return pltpu.make_async_remote_copy(
            src_ref=score_send,
            dst_ref=score_recv.at[source],
            send_sem=score_send_sem.at[target],
            recv_sem=score_recv_sem.at[source],
            device_id=place(target),
            device_id_type=pl.DeviceIdType.MESH,
        )

    fetches[7].wait()
    fetches[8].wait()
    pl.semaphore_wait(barrier, group - 1)
    for d in range(1, blocks):

        @pl.when(pos + d < n)
        def _():
            window_copy(d).start()

        @pl.when(pos < d)
        def _():
            window[d] = jnp.zeros_like(window[d])

    rows = lax.broadcasted_iota(jnp.int32, (frames, frames), 0)
    cols = lax.broadcasted_iota(jnp.int32, (frames, frames), 1)
    lower = rows >= cols
    strict = rows > cols
    tri = jnp.where(lower, 1.0, 0.0).astype(F32)
    eye = jnp.where(rows == cols, 1.0, 0.0).astype(F32)

    for i in (3, 4, 1, 0, 2):
        fetches[i].wait()
    gates = jnp.concatenate([g_ref[0], b_ref[0]], axis=0)
    sum_rows = exact(gates, tri, NT)
    sum_cols = exact(tri, gates, NT)
    gate_cols = exact(eye, gates, NT)
    q_all = q_ref[0].astype(F32)
    k_all = k_ref[0].astype(F32)
    v_all = v_ref[0].astype(F32)
    strict_parts = []
    for h in range(heads):
        kh = k_all[:, h, :]
        qh = q_all[:, h, :]
        rk = lax.rsqrt(jnp.sum(kh * kh, axis=-1, keepdims=True) + EPSILON)
        rq = lax.rsqrt(jnp.sum(qh * qh, axis=-1, keepdims=True) + EPSILON)
        kn = kh * rk
        qn = qh * rq
        kn_s[h] = kn
        qn_s[h] = qn
        col_s[h, :, 0:1] = rk
        col_s[h, :, 1:2] = rq
        c_col = sum_cols[:, h : h + 1]
        c_row = sum_rows[h : h + 1, :]
        beta = gate_cols[:, heads + h : heads + h + 1]
        last = c_col[frames - 1 : frames, :]
        lead = jnp.exp(c_col)
        tail = jnp.exp(last - c_col)
        col_s[h, :, 2:3] = beta
        col_s[h, :, 3:4] = lead
        col_s[h, :, 4:5] = tail
        m = jnp.where(lower, jnp.exp(jnp.where(lower, c_col - c_row, 0.0)), 0.0)
        m_s[h] = m
        both = PREP(jnp.concatenate([kn, qn], axis=0), kn, NT)
        l_mat = jnp.where(strict, beta * m * both[:frames], 0.0)
        l_s[h] = l_mat
        p_s[h] = m * both[frames:]
        strict_parts.append(l_mat)
    inverses = unit_lower_inverse(strict_parts, eye)
    for h in range(heads):
        a = inverses[h]
        a_s[h] = a
        kn = kn_s[h]
        beta = col_s[h, :, 2:3]
        lead = col_s[h, :, 3:4]
        tail = col_s[h, :, 4:5]
        wu = PREP(a, jnp.concatenate([beta * lead * kn, beta * v_all[:, h, :]], axis=1), NN)
        w_s[h] = wu[:, :width]
        u_s[h] = wu[:, width:]
        tk = tail * kn
        ends = PREP(tk, wu, TN)
        state_map = lead[frames - 1 : frames, :] * eye - ends[:, :width]
        map_s[h] = state_map
        map_t_s[h] = state_map.T
        shift_s[h] = ends[:, width:]
        inner = PREP(p_s[h], wu, NN)
        qt_s[h] = lead * qn_s[h] - inner[:, :width]
        y0_s[h] = inner[:, width:]
        z_s[h] = PREP(a, tk, TN)

    for i in (10, 5, 6, 9):
        fetches[i].wait()
    mask_row = mask_ref[...].astype(F32)
    mask_col = exact(eye, jnp.broadcast_to(mask_row, (8, frames)), NT)[:, 0:1]
    own_s[:, 0:1] = mask_col
    scale = width ** (-0.5)

    def attention():
        for d in range(1, blocks):

            @pl.when(pos >= d)
            def _():
                pltpu.make_async_copy(
                    window.at[d], window.at[d], win_recv_sem.at[d]
                ).wait()

        keys = window[:, 0].reshape(blocks * frames, width)
        values = window[:, 1].reshape(blocks * frames, width)
        t_pos = lax.broadcasted_iota(jnp.int32, (frames, blocks * frames), 0)
        slot = lax.broadcasted_iota(jnp.int32, (frames, blocks * frames), 1)
        distance = slot // frames
        j_pos = slot % frames - distance * frames
        allowed = (j_pos <= t_pos) & (j_pos > t_pos - WIN) & (distance <= pos)
        aq_all = aq_ref[0].astype(F32)
        ro_all = ro_ref[0].astype(F32)
        grad_k = jnp.zeros((blocks * frames, width), F32)
        grad_v = jnp.zeros((blocks * frames, width), F32)
        row_total = jnp.zeros((frames, 1), F32)
        for h in range(heads):
            aq = aq_all[:, h, :].astype(BF16)
            low = (ro_all[:, h, :] * mask_col)
            s = quick(aq, keys, NT) * scale
            s = jnp.where(allowed, s, -jnp.inf)
            e = jnp.exp(s - jnp.max(s, axis=-1, keepdims=True))
            soft = e / jnp.sum(e, axis=-1, keepdims=True)
            weights = soft.astype(BF16)
            out = quick(weights, values, NN)
            row_term = jnp.sum(low * out, axis=-1, keepdims=True)
            row_total = row_total + row_term
            grad_prob = quick(low, values, NT)
            grad_score = (soft * (grad_prob - row_term) * scale).astype(BF16)
            aq_grad_s[h] = quick(grad_score, keys, NN)
            grad_k = grad_k + quick(grad_score, aq, TN)
            grad_v = grad_v + quick(weights, low, TN)
        row_s[...] = jnp.broadcast_to(row_total, row_s.shape)
        own_s[:, width : 2 * width] = grad_k[:frames]
        own_s[:, 2 * width :] = grad_v[:frames]
        for d in range(1, blocks):

            @pl.when(pos >= d)
            def _():
                back_send[d - 1, 0] = grad_k[d * frames : (d + 1) * frames].astype(BF16)
                back_send[d - 1, 1] = grad_v[d * frames : (d + 1) * frames].astype(BF16)
                back_copy(d).start()

    late = pos * 2 >= n
    pl.when(late)(attention)

    for h in range(heads):

        @pl.when(pos == 0)
        def _():
            state_s[h] = s0_ref[0, h]

        @pl.when(pos > 0)
        def _():
            state_copy(h).wait_recv()
            state_s[h] = state_recv[h]

        @pl.when(pos < n - 1)
        def _():
            state_send[h] = shift_s[h] + RELAY(map_s[h], state_s[h], NN)
            state_copy(h).start()

    ro_all = ro_ref[0].astype(F32)
    gdn_rows = jnp.zeros((frames, 1), F32)
    for h in range(heads):
        raw = y0_s[h] + BACK(qt_s[h], state_s[h], NN)
        norm = lax.rsqrt(jnp.mean(raw * raw, axis=-1, keepdims=True) + EPSILON)
        out = raw * norm
        grad = ro_all[:, h, :] * mask_col
        along = jnp.sum(out * grad, axis=-1, keepdims=True)
        gdn_rows = gdn_rows + along
        g_raw = norm * (grad - out * (along * (1.0 / width)))
        g_s[h] = g_raw
        local_s[h] = BACK(qt_s[h], g_raw, TN)

        @pl.when(pos == n - 1)
        def _():
            next_s[h] = jnp.zeros_like(next_s[h])
            grad_send[h] = local_s[h]
            grad_copy(h).start()

    pl.when(jnp.logical_not(late))(attention)

    slot = slot_ref[0]
    sign = 1.0 - 2.0 * (slot % 2).astype(F32)
    tile_pair = lax.broadcasted_iota(jnp.int32, (8, 128), 1)
    member = jnp.where(tile_pair == slot // 2, 1.0, 0.0).astype(F32)
    score = jnp.sum(gdn_rows + row_s[:, 0:1], axis=0, keepdims=True) * total_frames ** (-0.5)
    contribution = member * sign * score
    score_send[...] = contribution
    score_recv[me] = contribution

    def post(j, c):
        score_copy(me, lax.rem(me + j, group)).start()
        return c

    lax.fori_loop(1, group, post, 0)

    for h in range(heads):

        @pl.when((pos < n - 1) & (pos > 0))
        def _():
            grad_copy(h).wait_recv()
            next_s[h] = grad_recv[h]
            grad_send[h] = local_s[h] + RELAY(map_t_s[h], next_s[h], NN)
            grad_copy(h).start()

    for h in range(heads):
        kn = kn_s[h]
        qn = qn_s[h]
        lead = col_s[h, :, 3:4]
        g_raw = g_s[h]
        state = state_s[h]
        delta = u_s[h] - BACK(w_s[h], state, NN)
        delta_s[h] = delta
        b0_s[h] = BACK(a_s[h], BACK(p_s[h], g_raw, TN), TN)
        dp = BACK(g_raw, delta, NT)
        dqk = dp * m_s[h]
        x1 = lead * BACK(g_raw, state, NT)
        dqn = quick(dqk, kn, NN) + x1
        n_mat = dp * p_s[h]
        local = col_s[h, :, 1:2] * (dqn - qn * jnp.sum(qn * dqn, axis=-1, keepdims=True))
        dq_s[h] = local
        a_s[h] = quick(dqk, qn, TN)
        p_s[h] = n_mat
        col_s[h, :, 5:6] = jnp.sum(x1 * qn, axis=-1, keepdims=True)

    for h in range(heads):

        @pl.when(pos == 0)
        def _():
            grad_copy(h).wait_recv()
            next_s[h] = grad_recv[h]

    def take(j, c):
        score_copy(lax.rem(me + j, group), lax.rem(me + j, group)).wait_recv()
        return c

    lax.fori_loop(1, group, take, 0)
    margin_count = margin_ref.shape[1]
    margin = jnp.sum(score_recv[...], axis=0)[0:1, :margin_count] - margin_ref[...]
    loss = jnp.maximum(-margin, 0.0) + jnp.log1p(jnp.exp(-jnp.abs(margin)))
    loss_ref[...] = jnp.sum(loss, axis=1, keepdims=True)
    pressure = jnp.sum(
        member[0:1, :margin_count] * (1.0 / (1.0 + jnp.exp(margin))), axis=1, keepdims=True
    )
    grad_scale = (total_frames * heads * halves * width) ** 0.5
    coefficient = -grad_scale * sign * pressure * total_frames ** (-0.5)

    dk_list = []
    dv_list = []
    dc_cols = []
    db_cols = []
    n_rows = []
    for h in range(heads):
        kn = kn_s[h]
        rk = col_s[h, :, 0:1]
        beta = col_s[h, :, 2:3]
        lead = col_s[h, :, 3:4]
        tail = col_s[h, :, 4:5]
        later = next_s[h]
        state = state_s[h]
        delta = delta_s[h]
        db = b0_s[h] + BACK(z_s[h], later, NN)
        dl = jnp.where(strict, -BACK(db, delta, NT), 0.0)
        l_term = dl * l_s[h]
        n_mat = p_s[h] + l_term
        dkk = dl * (beta * m_s[h])
        kb = lead * BACK(db, state, NT)
        x2 = -beta * kb
        x3 = tail * BACK(delta, later, NT)
        dkn = a_s[h] + x2 + x3 + quick(dkk, kn, NN) + quick(dkk, kn, TN)
        v_h = v_ref[0].astype(F32)[:, h, :]
        dk_list.append(rk * (dkn - kn * jnp.sum(kn * dkn, axis=-1, keepdims=True)))
        dv_list.append(beta * db)
        db_cols.append(
            jnp.sum(db * v_h - kb * kn, axis=-1, keepdims=True)
            + jnp.sum(l_term, axis=-1, keepdims=True) / beta
        )
        tail_term = jnp.sum(x3 * kn, axis=-1, keepdims=True)
        end_term = jnp.sum(tail_term, axis=0, keepdims=True) + lead[
            frames - 1 : frames, :
        ] * jnp.sum(jnp.sum(later * state, axis=-1, keepdims=True), axis=0, keepdims=True)
        dc = (
            jnp.sum(n_mat, axis=-1, keepdims=True)
            + col_s[h, :, 5:6]
            + jnp.sum(x2 * kn, axis=-1, keepdims=True)
            - tail_term
        )
        dc = dc + jnp.where(rows[:, 0:1] == frames - 1, end_term, 0.0)
        dc_cols.append(dc)
        n_rows.append(jnp.sum(n_mat, axis=0, keepdims=True))
    cols_all = jnp.concatenate(dc_cols + db_cols, axis=1)
    pad = [jnp.zeros((heads, frames), F32)]
    n_all = jnp.concatenate(n_rows + pad, axis=0)
    dg = (exact(cols_all, tri, TN) - exact(n_all, tri, NN))[:heads]
    dbeta = exact(cols_all, eye, TN)[heads:]
    dg_ref[0] = coefficient * dg
    db_ref[0] = coefficient * dbeta
    dq_ref[0] = jnp.stack([dq_s[h] * coefficient for h in range(heads)], axis=1).astype(BF16)
    dk_ref[0] = jnp.stack([x * coefficient for x in dk_list], axis=1).astype(BF16)
    dv_ref[0] = jnp.stack([x * coefficient for x in dv_list], axis=1).astype(BF16)
    daq_ref[0] = jnp.stack(
        [aq_grad_s[h] * coefficient for h in range(heads)], axis=1
    ).astype(BF16)

    for d in range(1, blocks):

        @pl.when(pos + d < n)
        def _():
            pltpu.make_async_copy(
                back_recv.at[d - 1], back_recv.at[d - 1], back_recv_sem.at[d]
            ).wait()
            own_s[:, width : 2 * width] += back_recv[d - 1, 0].astype(F32)
            own_s[:, 2 * width :] += back_recv[d - 1, 1].astype(F32)

    dak_ref[...] = (own_s[:, width : 2 * width] * coefficient).astype(BF16)
    dav_ref[...] = (own_s[:, 2 * width :] * coefficient).astype(BF16)

    for d in range(1, blocks):

        @pl.when(pos + d < n)
        def _():
            window_copy(d).wait_send()

        @pl.when(pos >= d)
        def _():
            back_copy(d).wait_send()

    for h in range(heads):

        @pl.when(pos < n - 1)
        def _():
            state_copy(h).wait_send()

        @pl.when(pos > 0)
        def _():
            grad_copy(h).wait_send()

    def sent(j, c):
        score_copy(me, lax.rem(me + j, group)).wait_send()
        return c

    lax.fori_loop(1, group, sent, 0)


def entry(sizes, *refs):
    sources, small = refs[:11], refs[11:13]
    results, rest = refs[13:22], refs[22:]
    held, fetch_sem, scratch = rest[:9], rest[9], rest[10:]
    window = scratch[0]
    targets = list(held[:7]) + [window.at[0, 0], window.at[0, 1]] + list(held[7:])
    copies = [
        pltpu.make_async_copy(source, target, fetch_sem.at[i])
        for i, (source, target) in enumerate(zip(sources, targets))
    ]
    for i in FETCH_ORDER:
        copies[i].start()
    kernel(sizes, copies, *held, *small, *results, *scratch)


def hand_over(*refs):
    count = (len(refs) - 2) // 3
    into, away = refs[-2:]
    held = refs[2 * count : 3 * count]
    taken = [pltpu.make_async_copy(refs[i], held[i], into.at[i]) for i in range(count)]
    given = [pltpu.make_async_copy(held[i], refs[count + i], away.at[i]) for i in range(count)]
    for copy in taken:
        copy.start()
    for first, second in zip(taken, given):
        first.wait()
        second.start()
    for copy in given:
        copy.wait()


FETCH_ORDER = (7, 8, 3, 4, 1, 0, 2, 10, 5, 6, 9)


def body(
    sizes,
    gdn_query,
    gdn_key,
    gdn_value,
    log_decay,
    write_rate,
    init_state,
    attn_query,
    attn_key,
    attn_value,
    readout,
    speaker_mask,
    pair_slot,
    ref_margin,
):
    n, pairs, halves = sizes
    group = n * pairs * halves
    seq, frames, heads, width = gdn_query.shape
    blocks = min(WIN // frames, n - 1) + 1
    vmem = pl.BlockSpec(memory_space=pltpu.VMEM)
    hbm = pl.BlockSpec(memory_space=pltpu.HBM)
    smem = pl.BlockSpec(memory_space=pltpu.SMEM)
    dma = pltpu.SemaphoreType.DMA
    square = pltpu.VMEM((heads, frames, width), F32)
    state_square = pltpu.VMEM((heads, width, width), F32)
    shape = jax.ShapeDtypeStruct
    out = pl.pallas_call(
        functools.partial(entry, sizes),
        out_shape=(
            shape((1, 1), F32),
            shape(gdn_query.shape, BF16),
            shape(gdn_key.shape, BF16),
            shape(gdn_value.shape, BF16),
            shape(log_decay.shape, F32),
            shape(write_rate.shape, F32),
            shape(attn_query.shape, BF16),
            shape((frames, width), BF16),
            shape((frames, width), BF16),
        ),
        in_specs=[hbm] * 11 + [smem, vmem],
        out_specs=(vmem,) * 9,
        scratch_shapes=[pltpu.VMEM(gdn_query.shape, BF16)] * 3
        + [pltpu.VMEM(log_decay.shape, F32)] * 2
        + [
            pltpu.VMEM(init_state.shape, F32),
            pltpu.VMEM(attn_query.shape, BF16),
            pltpu.VMEM(readout.shape, BF16),
            pltpu.VMEM(speaker_mask.shape, jnp.int32),
            dma((11,)),
            pltpu.VMEM((blocks, 2, frames, width), BF16),
            pltpu.VMEM((blocks - 1, 2, frames, width), BF16),
            pltpu.VMEM((blocks - 1, 2, frames, width), BF16),
            state_square,
            state_square,
            state_square,
            state_square,
            pltpu.VMEM((8, 128), F32),
            pltpu.VMEM((group, 8, 128), F32),
        ]
        + [square] * 14
        + [pltpu.VMEM((heads, frames, 128), F32)]
        + [square] * 8
        + [pltpu.VMEM((frames, 3 * width), F32), pltpu.VMEM((frames, 128), F32)]
        + [
            dma((blocks,)),
            dma((blocks,)),
            dma((blocks,)),
            dma((blocks,)),
            dma((heads,)),
            dma((heads,)),
            dma((heads,)),
            dma((heads,)),
            dma((group,)),
            dma((group,)),
        ],
        compiler_params=pltpu.CompilerParams(
            collective_id=0, has_side_effects=True, vmem_limit_bytes=62 * 1024 * 1024
        ),
    )(
        gdn_query,
        gdn_key,
        gdn_value,
        log_decay,
        write_rate,
        init_state,
        attn_query,
        attn_key.reshape(frames, width),
        attn_value.reshape(frames, width),
        readout,
        speaker_mask,
        pair_slot,
        ref_margin.reshape(1, -1),
    )
    final = pl.pallas_call(
        hand_over,
        out_shape=tuple(shape(a.shape, a.dtype) for a in out[1:]),
        in_specs=[hbm] * 8,
        out_specs=(hbm,) * 8,
        scratch_shapes=[pltpu.VMEM(a.shape, a.dtype) for a in out[1:]] + [dma((8,)), dma((8,))],
        compiler_params=pltpu.CompilerParams(vmem_limit_bytes=62 * 1024 * 1024),
    )(*out[1:])
    return (
        (out[0].reshape(1),)
        + tuple(final[:6])
        + (final[6].reshape(attn_key.shape), final[7].reshape(attn_value.shape))
    )


def solution(mesh):
    sizes = (mesh.shape["tm"], mesh.shape["pair"], mesh.shape["head"])
    wide = P(("groups", "pair"), "tm", "head", None)
    gate = P(("groups", "pair"), "head", "tm")
    return jax.shard_map(
        functools.partial(body, sizes),
        mesh=mesh,
        in_specs=(
            wide,
            wide,
            wide,
            gate,
            gate,
            P(("groups", "pair"), "head", None, None),
            wide,
            wide,
            wide,
            wide,
            P(("groups", "pair"), "tm"),
            P(("groups", "pair")),
            P("groups"),
        ),
        out_specs=(P("groups"), wide, wide, wide, gate, gate, wide, wide, wide),
        check_vma=False,
    )
```
